32 devices in a mesh: dp: 1, expert: 32 (over z, y, x, core).
Axes of the slice: x: 2, y: 2, z: 4, core: 2. Of those that a mesh axis runs over, the one named last changes fastest.
Arguments:
- tokens_in: bfloat16 [512, 2048], P(('dp', 'expert')), may hold values from -6 to 6
- out_grad: bfloat16 [512, 2048], P(('dp', 'expert')), may hold values from -6 to 6
- chosen: int32 [1, 16, 64], P('dp'), may hold values from 0 to 511, as said below
- counts: int32 [1, 16], P('dp'), may hold values from 48 to 64, as said below
- gates: bfloat16 [1, 16, 64], P('dp'), may hold values from 0.049804688 to 1
- w_up: bfloat16 [32, 2048, 2048], P('expert', None, 'dp'), may hold values from -0.125 to 0.125
- w_down: bfloat16 [32, 2048, 2048], P('expert', 'dp'), may hold values from -0.09375 to 0.09375
Outputs:
- in_grad: bfloat16 [512, 2048], P(('dp', 'expert'))
- grad_up: bfloat16 [32, 2048, 2048], P('expert', None, 'dp')
- grad_down: bfloat16 [32, 2048, 2048], P('expert', 'dp')
- gate_grad: float32 [1, 32, 32], P('dp', 'expert')
The draws below stay inside these ranges and needn't reach their ends.
Inputs may be any that keep to these rules, and one draw needn't show every extreme that they name: chosen[g, e, c] numbers a token within group g; that token lives on index chosen[g, e, c] // 16 of the expert axis. One list names no token twice. Among the first 32 slots of a list no two tokens live on the same index of the expert axis, nor among the last 32; so one expert takes at most 2 tokens of one device, and some device gives 2 to an expert in every list. Slots at or beyond counts[g, e] are ignored. `counts`: in every group some expert has all its slots valid.
All inputs are finite; a program needn't handle non-finite values.
Results may differ from the reference program's by a relative error of at most 0.028.
Values may be sent and summed in bfloat16 or wider, within the bound.
A program may use at most 64 MiB of HBM per device.

```python
import math
import jax
import jax.numpy as jnp
from jax import lax

D = 2048
FF = 4096
TOK_DEV = 16
OWNERS = 32
EXPERTS = 16
GROUPS = 1
CAP = 64
HIDDEN_DEV = 2048
TOKENS = 512
N_DP = 1


def one_list(list_key):
    half_cap = CAP // 2
    subkeys = jax.random.split(list_key, 5)
    order_one = jax.random.permutation(subkeys[0], OWNERS).astype(jnp.int32)
    order_two = jax.random.permutation(subkeys[1], OWNERS).astype(jnp.int32)
    spot_index = jax.random.randint(subkeys[2], (), 0, CAP // 4)
    target = order_one[spot_index]
    positions = jnp.arange(OWNERS, dtype=jnp.int32)
    order_two = jnp.where(order_two == target, order_two[spot_index], jnp.where(positions == spot_index, target, order_two))
    local_one = jax.random.randint(subkeys[3], (OWNERS,), 0, TOK_DEV)
    offset = jax.random.randint(subkeys[4], (OWNERS,), 1, TOK_DEV)
    local_two = (local_one + offset) % TOK_DEV
    front_owner = order_one[:half_cap]
    back_owner = order_two[:half_cap]
    front_rows = front_owner * TOK_DEV + local_one[front_owner]
    back_rows = back_owner * TOK_DEV + local_two[back_owner]
    return jnp.concatenate([front_rows, back_rows]).astype(jnp.int32)


def draw_chosen(key, part):
    subkeys = jax.random.split(jax.random.fold_in(key, 11), GROUPS * EXPERTS)
    all_lists = jax.vmap(one_list)(subkeys)
    return all_lists.reshape(GROUPS, EXPERTS, CAP).astype(jnp.int32)


def draw_counts(key, part):
    subkeys = jax.random.split(jax.random.fold_in(key, 23), 2)
    drawn = jax.random.randint(subkeys[0], (GROUPS, EXPERTS), CAP - CAP // 4, CAP + 1)
    full_expert = jax.random.randint(subkeys[1], (GROUPS, 1), 0, EXPERTS)
    expert_ids = jnp.arange(EXPERTS, dtype=jnp.int32)[None, :]
    return jnp.where(expert_ids == full_expert, CAP, drawn).astype(jnp.int32)


def level_of(own_key, dims, cuts, smallest, largest):
    level = 1.0
    for dim, blocks in cuts:
        draws = jax.random.uniform(jax.random.fold_in(jax.random.fold_in(own_key, 6), dim), (blocks,), jnp.float32, smallest / len(cuts), largest / len(cuts))
        level = level * jnp.repeat(jnp.exp(draws), dims[dim] // blocks).reshape((-1,) + (1,) * (len(dims) - 1 - dim))
    return level


def scatter_about(own_key, dims, width, most, cuts=(), kind=jnp.bfloat16):
    factor_of = level_of(own_key, dims, cuts, -0.22, 0.18) if cuts else 1.0
    result = jax.random.normal(own_key, dims, jnp.float32) * width * factor_of
    return jnp.minimum(jnp.maximum(result, -most), most).astype(kind)


def setup_inputs(seed: int = 0) -> dict:
    splits = jax.random.split(jax.random.key(seed), 8)
    tokens_in = scatter_about(splits[0], (TOKENS, D), 1.0, 6.0, ((0, 32),))
    out_grad = scatter_about(splits[1], (TOKENS, D), 1.0, 6.0, ((0, 32),))
    chosen = draw_chosen(jax.random.fold_in(splits[7], 71), 0)
    counts = draw_counts(jax.random.fold_in(splits[7], 71), 0)
    gates = jnp.clip(jnp.exp(jax.random.uniform(splits[4], (GROUPS, EXPERTS, CAP), jnp.float32, math.log(0.049804688), math.log(1.0))), 0.049804688, 1.0).astype(jnp.bfloat16)
    w_up = scatter_about(splits[5], (2 * EXPERTS, D, FF // 2), D ** -0.5, 0.125, ((0, 32),))
    w_down = scatter_about(splits[6], (2 * EXPERTS, FF // 2, D), FF ** -0.5, 0.09375, ((0, 32),))
    return {"tokens_in": tokens_in, "out_grad": out_grad, "chosen": chosen, "counts": counts, "gates": gates, "w_up": w_up, "w_down": w_down}


root_two_over_pi = 0.7978845608028654
cubic_coef = 0.044715


def gelu_pair(pre_act):
    inner_arg = root_two_over_pi * (pre_act + cubic_coef * pre_act * pre_act * pre_act)
    tangent = jnp.tanh(inner_arg)
    act_value = 0.5 * pre_act * (1.0 + tangent)
    act_slope = 0.5 * (1.0 + tangent) + 0.5 * pre_act * (1.0 - tangent * tangent) * root_two_over_pi * (1.0 + 3.0 * cubic_coef * pre_act * pre_act)
    return act_value, act_slope


def to_low(values):
    return lax.optimization_barrier(values.astype(jnp.bfloat16)).astype(jnp.float32)


def reference(tokens_in, out_grad, chosen, counts, gates, w_up, w_down):
    group_size = TOK_DEV * OWNERS
    slices = 2 * N_DP
    offsets = (jnp.arange(GROUPS, dtype=jnp.int32) * group_size)[:, None]
    slot_ids = jnp.arange(CAP, dtype=jnp.int32)[None, :]

    def per_expert(grad_acc, expert):
        row_ids = (chosen[:, expert, :] + offsets).astype(jnp.int32)
        is_valid = slot_ids < counts[:, expert][:, None]
        valid_float = is_valid.astype(jnp.float32)
        weight = jnp.where(is_valid, gates[:, expert, :].astype(jnp.float32), jnp.zeros((), jnp.float32))
        token_rows = tokens_in[row_ids].astype(jnp.float32)
        grad_rows = out_grad[row_ids].astype(jnp.float32)
        up_full = jnp.concatenate([w_up[2 * expert], w_up[2 * expert + 1]], axis=1).astype(jnp.float32)
        down_full = jnp.concatenate([w_down[2 * expert], w_down[2 * expert + 1]], axis=0).astype(jnp.float32)
        pre_act = jnp.einsum("gcd,df->gcf", token_rows, up_full)
        act_value, act_slope = gelu_pair(pre_act)
        hidden = to_low(act_value)
        back_grad = jnp.einsum("gcd,fd->gcf", grad_rows, down_full)
        scaled = to_low(weight[:, :, None] * grad_rows)
        pre_grad = to_low(weight[:, :, None] * back_grad * act_slope)
        grad_down = jnp.einsum("gcf,gcd->fd", hidden, scaled).astype(jnp.bfloat16)
        grad_up = jnp.einsum("gcd,gcf->df", token_rows, pre_grad).astype(jnp.bfloat16)
        split_grad = pre_grad.reshape(GROUPS, CAP, slices, HIDDEN_DEV)
        split_up = up_full.reshape(D, slices, HIDDEN_DEV)
        pieces = to_low(jnp.einsum("gcsh,dsh->gcsd", split_grad, split_up))
        contrib = jnp.sum(pieces, axis=2) * valid_float[:, :, None]
        gate_pieces = to_low(jnp.sum((hidden * back_grad).reshape(GROUPS, CAP, slices, HIDDEN_DEV), axis=3))
        gate_grad = jnp.sum(gate_pieces, axis=2) * valid_float
        grad_acc = grad_acc.at[row_ids.reshape(-1)].add(contrib.reshape(-1, D))
        up_halves = jnp.transpose(grad_up.reshape(D, 2, FF // 2), (1, 0, 2))
        down_halves = grad_down.reshape(2, FF // 2, D)
        return grad_acc, (up_halves, down_halves, gate_grad.reshape(GROUPS, 2, CAP // 2))

    start_acc = jnp.zeros((TOKENS, D), jnp.float32)
    grad_acc, (up_all, down_all, gate_all) = lax.scan(per_expert, start_acc, jnp.arange(EXPERTS, dtype=jnp.int32))
    in_grad = grad_acc.astype(jnp.bfloat16)
    grad_up = up_all.reshape(2 * EXPERTS, D, FF // 2)
    grad_down = down_all.reshape(2 * EXPERTS, FF // 2, D)
    gate_grad = jnp.transpose(gate_all, (1, 0, 2, 3)).reshape(GROUPS, 2 * EXPERTS, CAP // 2)
    return (in_grad, grad_up, grad_down, gate_grad)
```

```python
import functools
import jax
import jax.numpy as jnp
from jax import lax
from jax.experimental import pallas as pl
from jax.experimental.pallas import tpu as pltpu
from jax.sharding import PartitionSpec as P

root_two_over_pi = 0.7978845608028654
cubic_coef = 0.044715


def partner(x, axis, apart):
    return lax.ppermute(x, axis, [(i, i ^ 1 << apart) for i in range(lax.axis_size(axis))])


def gelu_pair(pre_act):
    inner_arg = root_two_over_pi * (pre_act + cubic_coef * pre_act * pre_act * pre_act)
    tangent = jnp.tanh(inner_arg)
    act_value = 0.5 * pre_act * (1.0 + tangent)
    act_slope = 0.5 * (1.0 + tangent) + 0.5 * pre_act * (
        1.0 - tangent * tangent
    ) * root_two_over_pi * (1.0 + 3.0 * cubic_coef * pre_act * pre_act)
    return (act_value, act_slope)


def on_device_any(tokens_in, out_grad, chosen, counts, gates, w_up, w_down):
    tok_local = tokens_in.shape[0]
    width = tokens_in.shape[1]
    owners = lax.axis_size("expert")
    groups = lax.axis_size("dp")
    capacity = chosen.shape[2]
    half_cap = capacity // 2
    num_experts = chosen.shape[1]
    device = lax.axis_index("expert")
    expert = device // 2
    parity = device % 2
    highest = lax.Precision.HIGHEST
    my_lists = chosen[0]
    slot_ids = jnp.arange(capacity, dtype=jnp.int32)
    is_valid = slot_ids[None, :] < counts[0][:, None]
    owner_of = my_lists // tok_local
    local_of = my_lists % tok_local
    mine = jnp.logical_and(owner_of == device, is_valid)
    local_ids = jnp.arange(tok_local, dtype=jnp.int32)
    hits = jnp.logical_and(mine[:, :, None], local_of[:, :, None] == local_ids[None, None, :])
    picked = jnp.sum(hits.astype(jnp.float32).reshape(num_experts, 2, half_cap, tok_local), axis=2)
    picked_low = picked.astype(jnp.bfloat16)
    list_row = lax.dynamic_index_in_dim(my_lists, expert, 0, keepdims=False)
    count_here = lax.dynamic_index_in_dim(counts[0], expert, 0, keepdims=False)
    valid_here = slot_ids < count_here
    gate_here = jnp.where(
        valid_here,
        lax.dynamic_index_in_dim(gates[0], expert, 0, keepdims=False),
        jnp.zeros((), jnp.bfloat16),
    )
    owner_ids = jnp.arange(owners, dtype=jnp.int32)
    slot_map = jnp.logical_and(
        (list_row // tok_local)[:, None] == owner_ids[None, :], valid_here[:, None]
    )
    slot_map = slot_map.astype(jnp.float32).reshape(2, half_cap, owners)
    map_low = slot_map.astype(jnp.bfloat16)
    gate_rows = gate_here.reshape(2, half_cap)
    send_x = jnp.einsum(
        "erl,ld->red", picked_low, tokens_in, preferred_element_type=jnp.float32
    ).astype(jnp.bfloat16)
    send_g = jnp.einsum(
        "erl,ld->red", picked_low, out_grad, preferred_element_type=jnp.float32
    ).astype(jnp.bfloat16)
    send_x = jnp.repeat(send_x, 2, axis=1)
    send_g = jnp.repeat(send_g, 2, axis=1)
    recv_x, recv_g = (
        lax.all_to_all(send_x, "expert", split_axis=1, concat_axis=1, tiled=True),
        lax.all_to_all(send_g, "expert", split_axis=1, concat_axis=1, tiled=True),
    )
    rows_x = jnp.einsum("rij,rjd->rid", map_low, recv_x, preferred_element_type=jnp.float32).astype(
        jnp.bfloat16
    )
    rows_g = jnp.einsum("rij,rjd->rid", map_low, recv_g, preferred_element_type=jnp.float32).astype(
        jnp.bfloat16
    )
    all_x, all_g, all_gate = (
        lax.all_gather(rows_x, "dp", axis=1, tiled=True),
        lax.all_gather(rows_g, "dp", axis=1, tiled=True),
        lax.all_gather(gate_rows, "dp", axis=1, tiled=True),
    )
    flat_x = all_x.reshape(-1, width)
    flat_g = all_g.reshape(-1, width)
    flat_gate = all_gate.reshape(-1).astype(jnp.float32)
    up_part = w_up[0]
    down_part = w_down[0]
    pre_act = jnp.dot(flat_x, up_part, preferred_element_type=jnp.float32)
    act_value, act_slope = gelu_pair(pre_act)
    hidden = act_value.astype(jnp.bfloat16)
    back_grad = lax.dot_general(
        flat_g, down_part, (((1,), (1,)), ((), ())), preferred_element_type=jnp.float32
    )
    gate_terms = jnp.sum(hidden.astype(jnp.float32) * back_grad, axis=1)
    scaled = (flat_gate[:, None] * flat_g.astype(jnp.float32)).astype(jnp.bfloat16)
    pre_grad = (flat_gate[:, None] * back_grad * act_slope).astype(jnp.bfloat16)
    grad_down = lax.dot_general(
        hidden, scaled, (((0,), (0,)), ((), ())), preferred_element_type=jnp.float32
    )
    grad_up = lax.dot_general(
        flat_x, pre_grad, (((0,), (0,)), ((), ())), preferred_element_type=jnp.float32
    )
    dx_terms = lax.dot_general(
        pre_grad, up_part, (((1,), (1,)), ((), ())), preferred_element_type=jnp.float32
    )
    hidden_sum, gate_sums = (
        lax.psum_scatter(
            dx_terms.reshape(2, groups * half_cap, width).astype(jnp.bfloat16),
            "dp",
            scatter_dimension=1,
            tiled=True,
        ).astype(jnp.float32),
        lax.psum_scatter(
            gate_terms.reshape(2, groups * half_cap).astype(jnp.bfloat16),
            "dp",
            scatter_dimension=1,
            tiled=True,
        ).astype(jnp.float32),
    )
    spread = jnp.einsum("rij,rid->rjd", slot_map, hidden_sum, precision=highest)
    returned = lax.all_to_all(
        spread.astype(jnp.bfloat16), "expert", split_axis=1, concat_axis=1, tiled=True
    ).astype(spread.dtype)
    take_back = jnp.repeat(picked, 2, axis=0)
    in_grad = jnp.einsum("krl,rkd->ld", take_back, returned, precision=highest)
    partner_gate = partner(gate_sums, "expert", 0)
    gate_total = gate_sums + partner_gate
    gate_out = lax.dynamic_index_in_dim(gate_total, parity, 0, keepdims=False).reshape(
        1, 1, half_cap
    )
    return (
        in_grad.astype(jnp.bfloat16),
        grad_up.astype(jnp.bfloat16)[None],
        grad_down.astype(jnp.bfloat16)[None],
        gate_out,
    )


NB = 8
HOP = 2 * NB


def is_one(cond):
    return jnp.where(cond, 1.0, 0.0)


def iota(shape, dim):
    return lax.broadcasted_iota(jnp.int32, shape, dim)


def f32_dot(a, b, dims=((1,), (0,))):
    return lax.dot_general(a, b, (dims, ((), ())), preferred_element_type=jnp.float32)


def expert_kernel(
    x_ref, g_ref, chosen_ref, counts_ref, gates_ref, up_hbm, down_hbm,
    in_grad_ref, gate_ref, rows_ref, scaled_ref, hidden_ref, pg_ref,
    up_v, down_v, send, recv, grows, slope, dx_acc, dx_out, dx_in, gate_out, gate_in,
    ret_send, ret_recv,
    w_sem, send_sem, recv_sem, fwd_send, fwd_recv, ret_ssem, ret_rsem, pair_send, pair_recv,
):
    tok, width = x_ref.shape
    experts, cap = chosen_ref.shape[1:]
    ff = up_v.shape[1]
    half = cap // 2
    wide = width // NB
    rows = 2 * experts
    log_tok = tok.bit_length() - 1
    me = lax.axis_index("expert")
    chip = me // 2
    core = me % 2
    mate = me + 1 - 2 * core

    up_copy = pltpu.make_async_copy(up_hbm.at[0], up_v, w_sem.at[0])
    down_copy = pltpu.make_async_copy(down_hbm.at[0], down_v, w_sem.at[1])
    up_copy.start()
    down_copy.start()

    def far(k):
        return lax.rem(chip + k, experts)

    barrier = pltpu.get_barrier_semaphore()
    pl.semaphore_signal(barrier, inc=1, device_id={"expert": mate})

    def greet(k, _):
        pl.semaphore_signal(barrier, inc=1, device_id={"expert": 2 * far(k) + core})
        return 0

    lax.fori_loop(1, experts, greet, 0)

    chosen = chosen_ref[0]
    slot = iota((experts, cap), 1)
    counts = counts_ref[...].astype(jnp.float32)
    diag = iota((experts, experts), 0) == iota((experts, experts), 1)
    count_col = jnp.sum(jnp.where(diag, counts, 0.0), axis=1, keepdims=True)
    local = chosen - me * tok
    mine = (local >= 0) & (local < tok) & (slot.astype(jnp.float32) < count_col)
    local_one = local.astype(jnp.float32) + 1.0
    lanes = NB * tok
    named = jnp.concatenate(
        [
            jnp.broadcast_to(
                jnp.sum(
                    jnp.where(mine & ((slot >= half) == bool(r)), local_one, 0.0),
                    axis=1, keepdims=True,
                ),
                (experts, lanes),
            )
            for r in range(2)
        ],
        axis=0,
    ).astype(jnp.bfloat16)
    tall = experts * HOP
    ti, tc = iota((tall, rows), 0), iota((tall, rows), 1)
    want = (ti & (HOP - 1)) // NB * experts + ti // HOP
    spread = is_one(want == tc).astype(jnp.bfloat16)
    full = f32_dot(spread, named)
    qi, ql = iota((tall, lanes), 0), iota((tall, lanes), 1)
    pick = is_one(
        (full == ((ql & (tok - 1)) + 1).astype(jnp.float32))
        & ((qi & (NB - 1)) == (ql >> log_tok))
    ).astype(jnp.bfloat16)

    pl.semaphore_wait(barrier, experts)

    for a, ref in enumerate((x_ref, g_ref)):
        stacked = jnp.concatenate(
            [ref[:, j * wide:(j + 1) * wide] for j in range(NB)], axis=0
        )
        packed = f32_dot(pick, stacked).astype(jnp.bfloat16)
        send[a] = packed.reshape(experts, HOP, wide)

        def push(k, _, a=a):
            dst = far(experts - k)
            pltpu.make_async_remote_copy(
                src_ref=send.at[a, dst],
                dst_ref=recv.at[a, core, chip],
                send_sem=send_sem.at[a, dst],
                recv_sem=recv_sem.at[a, chip],
                device_id={"expert": 2 * dst + core},
            ).start()
            return 0

        lax.fori_loop(1, experts, push, 0)
        recv[a, core, chip] = send[a, chip]

    pi, pc = iota((tall, tall), 0), iota((tall, tall), 1)
    unpack = is_one(
        pc == ((pi & (rows - 1)) >> 1) * HOP + (pi & 1) * NB + pi // rows
    ).astype(jnp.bfloat16)

    def arrive(a):
        def one(k, _):
            src = far(k)
            pltpu.make_async_remote_copy(
                src_ref=send.at[a, src],
                dst_ref=recv.at[a, core, src],
                send_sem=send_sem.at[a, src],
                recv_sem=recv_sem.at[a, src],
                device_id={"expert": 2 * src + core},
            ).wait()
            return 0

        lax.fori_loop(1, experts, one, 0)
        copy = pltpu.make_async_remote_copy(
            src_ref=recv.at[a, core],
            dst_ref=recv.at[a, core],
            send_sem=fwd_send.at[a],
            recv_sem=fwd_recv.at[a],
            device_id={"expert": mate},
        )
        copy.start()
        return copy

    def unfold(a, parity, out):
        flat = f32_dot(unpack, recv[a, parity].reshape(tall, wide)).astype(jnp.bfloat16)
        at = pl.ds(pl.multiple_of(parity * rows, rows), rows)
        for j in range(NB):
            out[at, j * wide:(j + 1) * wide] = flat[j * rows:(j + 1) * rows]

    def other_half(a):
        return pltpu.make_async_remote_copy(
            src_ref=recv.at[a, 1 - core],
            dst_ref=recv.at[a, 1 - core],
            send_sem=fwd_send.at[a],
            recv_sem=fwd_recv.at[a],
            device_id={"expert": mate},
        )

    my_list = chosen_ref[0, pl.ds(chip, 1), :]
    my_gate = gates_ref[0].astype(jnp.float32)
    my_gate = jnp.sum(
        jnp.where(iota((experts, cap), 0) == chip, my_gate, 0.0), axis=0, keepdims=True
    )
    my_count = jnp.sum(
        jnp.where(iota((1, experts), 1) == chip, counts, 0.0), axis=1, keepdims=True
    )
    owner = my_list >> log_tok
    late = jnp.where(iota((1, cap), 1) >= half, 1, 0)
    place = (owner & 1) * rows + (owner >> 1) * 2 + late
    live = iota((1, cap), 1).astype(jnp.float32) < my_count
    seat = is_one((iota((2 * rows, cap), 0) == place) & live)
    weight = jnp.sum(seat * my_gate, axis=1, keepdims=True)

    fwd_x = arrive(0)
    unfold(0, core, rows_ref)
    up_copy.wait()
    other_half(0).wait_recv()
    unfold(0, 1 - core, rows_ref)

    step = 512
    x_rows = rows_ref[...]

    def forward(c, _):
        cols = pl.ds(pl.multiple_of(c * step, step), step)
        value, tilt = gelu_pair(f32_dot(x_rows, up_v[:, cols]))
        hidden_ref[:, cols] = value.astype(jnp.bfloat16)
        slope[:, cols] = tilt
        return 0

    lax.fori_loop(0, ff // step, forward, 0)

    fwd_g = arrive(1)
    unfold(1, core, grows)
    down_copy.wait()
    other_half(1).wait_recv()
    unfold(1, 1 - core, grows)
    g_rows = grows[...]
    scaled_ref[...] = (weight * g_rows.astype(jnp.float32)).astype(jnp.bfloat16)
    dx_acc[...] = jnp.zeros_like(dx_acc)

    def backward(c, total):
        cols = pl.ds(pl.multiple_of(c * step, step), step)
        back = f32_dot(g_rows, down_v[cols, :], ((1,), (1,)))
        pre_grad = (weight * back * slope[:, cols]).astype(jnp.bfloat16)
        pg_ref[:, cols] = pre_grad
        dx_acc[...] += f32_dot(pre_grad, up_v[:, cols], ((1,), (1,)))
        return total + jnp.sum(
            hidden_ref[:, cols].astype(jnp.float32) * back, axis=1, keepdims=True
        )

    gate_terms = lax.fori_loop(
        0, ff // step, backward, jnp.zeros((2 * rows, 1), jnp.float32)
    )

    theirs = pl.ds(pl.multiple_of((1 - core) * rows, rows), rows)
    ours = pl.ds(pl.multiple_of(core * rows, rows), rows)
    dx_out[...] = dx_acc[theirs, :].astype(jnp.bfloat16)
    dx_copy = pltpu.make_async_remote_copy(
        src_ref=dx_out, dst_ref=dx_in,
        send_sem=pair_send.at[0], recv_sem=pair_recv.at[0], device_id={"expert": mate},
    )
    dx_copy.start()
    low = gate_terms.astype(jnp.bfloat16).astype(jnp.float32)
    by_slot = jnp.sum(seat * low, axis=0, keepdims=True)
    gate_out[...] = jnp.broadcast_to(
        jnp.concatenate([by_slot, jnp.zeros((1, 128 - cap), jnp.float32)], axis=1), (8, 128)
    )
    gate_copy = pltpu.make_async_remote_copy(
        src_ref=gate_out, dst_ref=gate_in,
        send_sem=pair_send.at[1], recv_sem=pair_recv.at[1], device_id={"expert": mate},
    )
    gate_copy.start()
    dx_copy.wait()
    both = (
        dx_acc[ours, :].astype(jnp.bfloat16).astype(jnp.float32)
        + dx_in[...].astype(jnp.float32)
    ).astype(jnp.bfloat16)
    stacked = jnp.concatenate([both[:, j * wide:(j + 1) * wide] for j in range(NB)], axis=0)
    packed = f32_dot(unpack, stacked, ((0,), (0,))).astype(jnp.bfloat16)
    ret_send[...] = packed.reshape(experts, HOP, wide)

    def give_back(k, _):
        dst = far(experts - k)
        pltpu.make_async_remote_copy(
            src_ref=ret_send.at[dst],
            dst_ref=ret_recv.at[chip],
            send_sem=ret_ssem.at[dst],
            recv_sem=ret_rsem.at[chip],
            device_id={"expert": 2 * dst + core},
        ).start()
        return 0

    lax.fori_loop(1, experts, give_back, 0)
    ret_recv[chip] = ret_send[chip]

    gate_copy.wait()
    total = gate_out[0:1, :cap] + gate_in[0:1, :cap]
    gate_ref[0] = jnp.where(core == 0, total[:, :half], total[:, half:])
    fwd_x.wait_send()
    fwd_g.wait_send()

    def taken(k, _):
        src = far(k)
        pltpu.make_async_remote_copy(
            src_ref=ret_send.at[src],
            dst_ref=ret_recv.at[src],
            send_sem=ret_ssem.at[src],
            recv_sem=ret_rsem.at[src],
            device_id={"expert": 2 * src + core},
        ).wait()
        return 0

    lax.fori_loop(1, experts, taken, 0)
    folded = f32_dot(pick, ret_recv[...].reshape(tall, wide), ((0,), (0,))).astype(jnp.bfloat16)
    for j in range(NB):
        in_grad_ref[:, j * wide:(j + 1) * wide] = folded[j * tok:(j + 1) * tok]


def grads_kernel(rows_ref, pg_ref, hidden_ref, scaled_ref, up_ref, down_ref):
    up_ref[0] = f32_dot(rows_ref[...], pg_ref[...], ((0,), (0,))).astype(jnp.bfloat16)
    down_ref[0] = f32_dot(hidden_ref[...], scaled_ref[...], ((0,), (0,))).astype(jnp.bfloat16)


def on_device_pairs(tokens_in, out_grad, chosen, counts, gates, w_up, w_down):
    tok, width = tokens_in.shape
    experts, cap = chosen.shape[1:]
    ff = w_up.shape[2]
    rows = 2 * experts
    wide = width // NB
    bf16, f32 = jnp.bfloat16, jnp.float32
    vmem = pl.BlockSpec(memory_space=pltpu.VMEM)
    hbm = pl.BlockSpec(memory_space=pl.ANY)
    dma = pltpu.SemaphoreType.DMA
    in_grad, gate_grad, x_rows, scaled, hidden, pre_grad = pl.pallas_call(
        expert_kernel,
        out_shape=(
            jax.ShapeDtypeStruct((tok, width), bf16),
            jax.ShapeDtypeStruct((1, 1, cap // 2), f32),
            jax.ShapeDtypeStruct((2 * rows, width), bf16),
            jax.ShapeDtypeStruct((2 * rows, width), bf16),
            jax.ShapeDtypeStruct((2 * rows, ff), bf16),
            jax.ShapeDtypeStruct((2 * rows, ff), bf16),
        ),
        in_specs=[vmem] * 5 + [hbm] * 2,
        out_specs=(vmem,) * 6,
        scratch_shapes=[
            pltpu.VMEM((width, ff), bf16),
            pltpu.VMEM((ff, width), bf16),
            pltpu.VMEM((2, experts, HOP, wide), bf16),
            pltpu.VMEM((2, 2, experts, HOP, wide), bf16),
            pltpu.VMEM((2 * rows, width), bf16),
            pltpu.VMEM((2 * rows, ff), f32),
            pltpu.VMEM((2 * rows, width), f32),
            pltpu.VMEM((rows, width), bf16),
            pltpu.VMEM((rows, width), bf16),
            pltpu.VMEM((8, 128), f32),
            pltpu.VMEM((8, 128), f32),
            pltpu.VMEM((experts, HOP, wide), bf16),
            pltpu.VMEM((experts, HOP, wide), bf16),
            dma((2,)),
            dma((2, experts)),
            dma((2, experts)),
            dma((2,)),
            dma((2,)),
            dma((experts,)),
            dma((experts,)),
            dma((2,)),
            dma((2,)),
        ],
        compiler_params=pltpu.CompilerParams(
            collective_id=0, has_side_effects=True, vmem_limit_bytes=40 << 20
        ),
        cost_estimate=pl.CostEstimate(
            flops=6 * 2 * rows * width * ff,
            bytes_accessed=4 * width * ff,
            transcendentals=2 * rows * ff,
        ),
    )(tokens_in, out_grad, chosen, counts, gates, w_up, w_down)

    steps = 8
    grad_up, grad_down = pl.pallas_call(
        grads_kernel,
        grid=(steps,),
        out_shape=(
            jax.ShapeDtypeStruct((1, width, ff), bf16),
            jax.ShapeDtypeStruct((1, ff, width), bf16),
        ),
        in_specs=[
            pl.BlockSpec((2 * rows, width // steps), lambda i: (0, i)),
            pl.BlockSpec((2 * rows, ff), lambda i: (0, 0)),
            pl.BlockSpec((2 * rows, ff // steps), lambda i: (0, i)),
            pl.BlockSpec((2 * rows, width), lambda i: (0, 0)),
        ],
        out_specs=(
            pl.BlockSpec((1, width // steps, ff), lambda i: (0, i, 0)),
            pl.BlockSpec((1, ff // steps, width), lambda i: (0, i, 0)),
        ),
        compiler_params=pltpu.CompilerParams(vmem_limit_bytes=32 << 20),
        cost_estimate=pl.CostEstimate(
            flops=8 * rows * width * ff,
            bytes_accessed=4 * width * ff,
            transcendentals=0,
        ),
    )(x_rows, pre_grad, hidden, scaled)
    return in_grad, grad_up, grad_down, gate_grad


def on_device(mesh, *args):
    tok, width = args[0].shape
    experts, cap = args[2].shape[1:]
    two = lambda v: v & (v - 1) == 0
    fits = (
        mesh.shape["dp"] == 1
        and mesh.shape["expert"] == 2 * experts
        and cap == 4 * experts
        and cap <= 128
        and tok % 16 == 0
        and width % 2048 == 0
        and args[5].shape[2] % 2048 == 0
        and two(tok)
        and two(experts)
    )
    return (on_device_pairs if fits else on_device_any)(*args)


def solution(mesh):
    placed = (
        P(("dp", "expert"), None),
        P(("dp", "expert"), None),
        P("dp", None, None),
        P("dp", None),
        P("dp", None, None),
        P("expert", None, "dp"),
        P("expert", "dp", None),
    )
    return jax.shard_map(
        functools.partial(on_device, mesh),
        mesh=mesh,
        in_specs=placed,
        out_specs=(
            P(("dp", "expert"), None),
            P("expert", None, "dp"),
            P("expert", "dp", None),
            P("dp", "expert", None),
        ),
        check_vma=False,
    )
```

```python
import functools
import jax
import jax.numpy as jnp
from jax import lax
from jax.experimental import pallas as pl
from jax.experimental.pallas import tpu as pltpu
from jax.sharding import PartitionSpec as P

root_two_over_pi = 0.7978845608028654
cubic_coef = 0.044715


def partner(x, axis, apart):
    return lax.ppermute(x, axis, [(i, i ^ 1 << apart) for i in range(lax.axis_size(axis))])


def gelu_pair(pre_act):
    inner_arg = root_two_over_pi * (pre_act + cubic_coef * pre_act * pre_act * pre_act)
    tangent = jnp.tanh(inner_arg)
    act_value = 0.5 * pre_act * (1.0 + tangent)
    act_slope = 0.5 * (1.0 + tangent) + 0.5 * pre_act * (
        1.0 - tangent * tangent
    ) * root_two_over_pi * (1.0 + 3.0 * cubic_coef * pre_act * pre_act)
    return (act_value, act_slope)


def on_device_any(tokens_in, out_grad, chosen, counts, gates, w_up, w_down):
    tok_local = tokens_in.shape[0]
    width = tokens_in.shape[1]
    owners = lax.axis_size("expert")
    groups = lax.axis_size("dp")
    capacity = chosen.shape[2]
    half_cap = capacity // 2
    num_experts = chosen.shape[1]
    device = lax.axis_index("expert")
    expert = device // 2
    parity = device % 2
    highest = lax.Precision.HIGHEST
    my_lists = chosen[0]
    slot_ids = jnp.arange(capacity, dtype=jnp.int32)
    is_valid = slot_ids[None, :] < counts[0][:, None]
    owner_of = my_lists // tok_local
    local_of = my_lists % tok_local
    mine = jnp.logical_and(owner_of == device, is_valid)
    local_ids = jnp.arange(tok_local, dtype=jnp.int32)
    hits = jnp.logical_and(mine[:, :, None], local_of[:, :, None] == local_ids[None, None, :])
    picked = jnp.sum(hits.astype(jnp.float32).reshape(num_experts, 2, half_cap, tok_local), axis=2)
    picked_low = picked.astype(jnp.bfloat16)
    list_row = lax.dynamic_index_in_dim(my_lists, expert, 0, keepdims=False)
    count_here = lax.dynamic_index_in_dim(counts[0], expert, 0, keepdims=False)
    valid_here = slot_ids < count_here
    gate_here = jnp.where(
        valid_here,
        lax.dynamic_index_in_dim(gates[0], expert, 0, keepdims=False),
        jnp.zeros((), jnp.bfloat16),
    )
    owner_ids = jnp.arange(owners, dtype=jnp.int32)
    slot_map = jnp.logical_and(
        (list_row // tok_local)[:, None] == owner_ids[None, :], valid_here[:, None]
    )
    slot_map = slot_map.astype(jnp.float32).reshape(2, half_cap, owners)
    map_low = slot_map.astype(jnp.bfloat16)
    gate_rows = gate_here.reshape(2, half_cap)
    send_x = jnp.einsum(
        "erl,ld->red", picked_low, tokens_in, preferred_element_type=jnp.float32
    ).astype(jnp.bfloat16)
    send_g = jnp.einsum(
        "erl,ld->red", picked_low, out_grad, preferred_element_type=jnp.float32
    ).astype(jnp.bfloat16)
    send_x = jnp.repeat(send_x, 2, axis=1)
    send_g = jnp.repeat(send_g, 2, axis=1)
    recv_x, recv_g = (
        lax.all_to_all(send_x, "expert", split_axis=1, concat_axis=1, tiled=True),
        lax.all_to_all(send_g, "expert", split_axis=1, concat_axis=1, tiled=True),
    )
    rows_x = jnp.einsum("rij,rjd->rid", map_low, recv_x, preferred_element_type=jnp.float32).astype(
        jnp.bfloat16
    )
    rows_g = jnp.einsum("rij,rjd->rid", map_low, recv_g, preferred_element_type=jnp.float32).astype(
        jnp.bfloat16
    )
    all_x, all_g, all_gate = (
        lax.all_gather(rows_x, "dp", axis=1, tiled=True),
        lax.all_gather(rows_g, "dp", axis=1, tiled=True),
        lax.all_gather(gate_rows, "dp", axis=1, tiled=True),
    )
    flat_x = all_x.reshape(-1, width)
    flat_g = all_g.reshape(-1, width)
    flat_gate = all_gate.reshape(-1).astype(jnp.float32)
    up_part = w_up[0]
    down_part = w_down[0]
    pre_act = jnp.dot(flat_x, up_part, preferred_element_type=jnp.float32)
    act_value, act_slope = gelu_pair(pre_act)
    hidden = act_value.astype(jnp.bfloat16)
    back_grad = lax.dot_general(
        flat_g, down_part, (((1,), (1,)), ((), ())), preferred_element_type=jnp.float32
    )
    gate_terms = jnp.sum(hidden.astype(jnp.float32) * back_grad, axis=1)
    scaled = (flat_gate[:, None] * flat_g.astype(jnp.float32)).astype(jnp.bfloat16)
    pre_grad = (flat_gate[:, None] * back_grad * act_slope).astype(jnp.bfloat16)
    grad_down = lax.dot_general(
        hidden, scaled, (((0,), (0,)), ((), ())), preferred_element_type=jnp.float32
    )
    grad_up = lax.dot_general(
        flat_x, pre_grad, (((0,), (0,)), ((), ())), preferred_element_type=jnp.float32
    )
    dx_terms = lax.dot_general(
        pre_grad, up_part, (((1,), (1,)), ((), ())), preferred_element_type=jnp.float32
    )
    hidden_sum, gate_sums = (
        lax.psum_scatter(
            dx_terms.reshape(2, groups * half_cap, width).astype(jnp.bfloat16),
            "dp",
            scatter_dimension=1,
            tiled=True,
        ).astype(jnp.float32),
        lax.psum_scatter(
            gate_terms.reshape(2, groups * half_cap).astype(jnp.bfloat16),
            "dp",
            scatter_dimension=1,
            tiled=True,
        ).astype(jnp.float32),
    )
    spread = jnp.einsum("rij,rid->rjd", slot_map, hidden_sum, precision=highest)
    returned = lax.all_to_all(
        spread.astype(jnp.bfloat16), "expert", split_axis=1, concat_axis=1, tiled=True
    ).astype(spread.dtype)
    take_back = jnp.repeat(picked, 2, axis=0)
    in_grad = jnp.einsum("krl,rkd->ld", take_back, returned, precision=highest)
    partner_gate = partner(gate_sums, "expert", 0)
    gate_total = gate_sums + partner_gate
    gate_out = lax.dynamic_index_in_dim(gate_total, parity, 0, keepdims=False).reshape(
        1, 1, half_cap
    )
    return (
        in_grad.astype(jnp.bfloat16),
        grad_up.astype(jnp.bfloat16)[None],
        grad_down.astype(jnp.bfloat16)[None],
        gate_out,
    )


NB = 8
HOP = 2 * NB


def is_one(cond):
    return jnp.where(cond, 1.0, 0.0)


def iota(shape, dim):
    return lax.broadcasted_iota(jnp.int32, shape, dim)


def f32_dot(a, b, dims=((1,), (0,))):
    return lax.dot_general(a, b, (dims, ((), ())), preferred_element_type=jnp.float32)


def expert_kernel(
    x_hbm, g_hbm, chosen_hbm, counts_hbm, gates_hbm, up_hbm, down_hbm,
    in_grad_ref, gate_ref, rows_hbm, scaled_hbm, hidden_hbm, pg_hbm,
    rows_ref, scaled_ref, hidden_ref, pg_ref, x_ref, g_ref, chosen_ref, counts_ref, gates_ref, up_v, down_v, send, recv, grows, slope, dx_acc, dx_out, dx_in, gate_out, gate_in,
    ret_send, ret_recv,
    in_sem, out_sem, w_sem, send_sem, recv_sem, fwd_send, fwd_recv, ret_ssem, ret_rsem, pair_send, pair_recv,
):
    tok, width = x_ref.shape
    experts, cap = chosen_ref.shape[1:]
    ff = up_v.shape[1]
    half = cap // 2
    wide = width // NB
    rows = 2 * experts
    log_tok = tok.bit_length() - 1
    me = lax.axis_index("expert")
    chip = me // 2
    core = me % 2
    mate = me + 1 - 2 * core

    small = [
        pltpu.make_async_copy(src, dst, in_sem.at[i])
        for i, (src, dst) in enumerate(
            (
                (chosen_hbm, chosen_ref),
                (counts_hbm, counts_ref),
                (x_hbm, x_ref),
                (g_hbm, g_ref),
                (gates_hbm, gates_ref),
            )
        )
    ]
    for copy in small:
        copy.start()
    up_copy = pltpu.make_async_copy(up_hbm.at[0], up_v, w_sem.at[0])
    down_copy = pltpu.make_async_copy(down_hbm.at[0], down_v, w_sem.at[1])
    up_copy.start()
    down_copy.start()

    def far(k):
        return lax.rem(chip + k, experts)

    barrier = pltpu.get_barrier_semaphore()
    pl.semaphore_signal(barrier, inc=1, device_id={"expert": mate})

    def greet(k, _):
        pl.semaphore_signal(barrier, inc=1, device_id={"expert": 2 * far(k) + core})
        return 0

    lax.fori_loop(1, experts, greet, 0)

    small[0].wait()
    small[1].wait()

    chosen = chosen_ref[0]
    slot = iota((experts, cap), 1)
    counts = counts_ref[...].astype(jnp.float32)
    diag = iota((experts, experts), 0) == iota((experts, experts), 1)
    count_col = jnp.sum(jnp.where(diag, counts, 0.0), axis=1, keepdims=True)
    local = chosen - me * tok
    mine = (local >= 0) & (local < tok) & (slot.astype(jnp.float32) < count_col)
    local_one = local.astype(jnp.float32) + 1.0
    lanes = NB * tok
    named = jnp.concatenate(
        [
            jnp.broadcast_to(
                jnp.sum(
                    jnp.where(mine & ((slot >= half) == bool(r)), local_one, 0.0),
                    axis=1, keepdims=True,
                ),
                (experts, lanes),
            )
            for r in range(2)
        ],
        axis=0,
    ).astype(jnp.bfloat16)
    tall = experts * HOP
    ti, tc = iota((tall, rows), 0), iota((tall, rows), 1)
    want = (ti & (HOP - 1)) // NB * experts + ti // HOP
    spread = is_one(want == tc).astype(jnp.bfloat16)
    full = f32_dot(spread, named)
    qi, ql = iota((tall, lanes), 0), iota((tall, lanes), 1)
    pick = is_one(
        (full == ((ql & (tok - 1)) + 1).astype(jnp.float32))
        & ((qi & (NB - 1)) == (ql >> log_tok))
    ).astype(jnp.bfloat16)

    small[2].wait()
    pl.semaphore_wait(barrier, experts)

    for a, ref in enumerate((x_ref, g_ref)):
        if a == 1:
            small[3].wait()
        stacked = jnp.concatenate(
            [ref[:, j * wide:(j + 1) * wide] for j in range(NB)], axis=0
        )
        packed = f32_dot(pick, stacked).astype(jnp.bfloat16)
        send[a] = packed.reshape(experts, HOP, wide)

        def push(k, _, a=a):
            dst = far(experts - k)
            pltpu.make_async_remote_copy(
                src_ref=send.at[a, dst],
                dst_ref=recv.at[a, core, chip],
                send_sem=send_sem.at[a],
                recv_sem=recv_sem.at[a],
                device_id={"expert": 2 * dst + core},
            ).start()
            return 0

        lax.fori_loop(1, experts, push, 0)
        recv[a, core, chip] = send[a, chip]

    pi, pc = iota((tall, tall), 0), iota((tall, tall), 1)
    unpack = is_one(
        pc == ((pi & (rows - 1)) >> 1) * HOP + (pi & 1) * NB + pi // rows
    ).astype(jnp.bfloat16)

    def arrive(a):
        every = pl.ds(0, experts - 1)
        pltpu.make_async_copy(
            recv.at[a, core, every], recv.at[a, core, every], recv_sem.at[a]
        ).wait()
        copy = pltpu.make_async_remote_copy(
            src_ref=recv.at[a, core],
            dst_ref=recv.at[a, core],
            send_sem=fwd_send.at[a],
            recv_sem=fwd_recv.at[a],
            device_id={"expert": mate},
        )
        copy.start()
        return copy

    def unfold(a, parity, out):
        flat = f32_dot(unpack, recv[a, parity].reshape(tall, wide)).astype(jnp.bfloat16)
        at = pl.ds(pl.multiple_of(parity * rows, rows), rows)
        for j in range(NB):
            out[at, j * wide:(j + 1) * wide] = flat[j * rows:(j + 1) * rows]

    def other_half(a):
        return pltpu.make_async_remote_copy(
            src_ref=recv.at[a, 1 - core],
            dst_ref=recv.at[a, 1 - core],
            send_sem=fwd_send.at[a],
            recv_sem=fwd_recv.at[a],
            device_id={"expert": mate},
        )

    small[4].wait()

    my_list = chosen_ref[0, pl.ds(chip, 1), :]
    my_gate = gates_ref[0].astype(jnp.float32)
    my_gate = jnp.sum(
        jnp.where(iota((experts, cap), 0) == chip, my_gate, 0.0), axis=0, keepdims=True
    )
    my_count = jnp.sum(
        jnp.where(iota((1, experts), 1) == chip, counts, 0.0), axis=1, keepdims=True
    )
    owner = my_list >> log_tok
    late = jnp.where(iota((1, cap), 1) >= half, 1, 0)
    place = (owner & 1) * rows + (owner >> 1) * 2 + late
    live = iota((1, cap), 1).astype(jnp.float32) < my_count
    seat = is_one((iota((2 * rows, cap), 0) == place) & live)
    weight = jnp.sum(seat * my_gate, axis=1, keepdims=True)

    fwd_x = arrive(0)
    unfold(0, core, rows_ref)
    up_copy.wait()
    other_half(0).wait_recv()
    unfold(0, 1 - core, rows_ref)

    step = 1024
    x_rows = rows_ref[...]

    def forward(c, _):
        cols = pl.ds(pl.multiple_of(c * step, step), step)
        value, tilt = gelu_pair(f32_dot(x_rows, up_v[:, cols]))
        hidden_ref[:, cols] = value.astype(jnp.bfloat16)
        slope[:, cols] = tilt
        return 0

    lax.fori_loop(0, ff // step, forward, 0)

    fwd_g = arrive(1)
    unfold(1, core, grows)
    down_copy.wait()
    other_half(1).wait_recv()
    unfold(1, 1 - core, grows)
    g_rows = grows[...]
    scaled_ref[...] = (weight * g_rows.astype(jnp.float32)).astype(jnp.bfloat16)
    dx_acc[...] = jnp.zeros_like(dx_acc)

    def backward(c, total):
        cols = pl.ds(pl.multiple_of(c * step, step), step)
        back = f32_dot(g_rows, down_v[cols, :], ((1,), (1,)))
        pre_grad = (weight * back * slope[:, cols]).astype(jnp.bfloat16)
        pg_ref[:, cols] = pre_grad
        dx_acc[...] += f32_dot(pre_grad, up_v[:, cols], ((1,), (1,)))
        return total + jnp.sum(
            hidden_ref[:, cols].astype(jnp.float32) * back, axis=1, keepdims=True
        )

    gate_terms = lax.fori_loop(
        0, ff // step, backward, jnp.zeros((2 * rows, 1), jnp.float32)
    )

    theirs = pl.ds(pl.multiple_of((1 - core) * rows, rows), rows)
    ours = pl.ds(pl.multiple_of(core * rows, rows), rows)
    dx_out[...] = dx_acc[theirs, :].astype(jnp.bfloat16)
    dx_copy = pltpu.make_async_remote_copy(
        src_ref=dx_out, dst_ref=dx_in,
        send_sem=pair_send.at[0], recv_sem=pair_recv.at[0], device_id={"expert": mate},
    )
    dx_copy.start()
    low = gate_terms.astype(jnp.bfloat16).astype(jnp.float32)
    by_slot = jnp.sum(seat * low, axis=0, keepdims=True)
    gate_out[...] = jnp.broadcast_to(
        jnp.concatenate([by_slot, jnp.zeros((1, 128 - cap), jnp.float32)], axis=1), (8, 128)
    )
    gate_copy = pltpu.make_async_remote_copy(
        src_ref=gate_out, dst_ref=gate_in,
        send_sem=pair_send.at[1], recv_sem=pair_recv.at[1], device_id={"expert": mate},
    )
    gate_copy.start()
    keep = [
        pltpu.make_async_copy(src, dst, out_sem.at[i])
        for i, (src, dst) in enumerate(
            (
                (rows_ref, rows_hbm),
                (scaled_ref, scaled_hbm),
                (hidden_ref, hidden_hbm),
                (pg_ref, pg_hbm),
            )
        )
    ]
    for copy in keep:
        copy.start()
    dx_copy.wait()
    both = (
        dx_acc[ours, :].astype(jnp.bfloat16).astype(jnp.float32)
        + dx_in[...].astype(jnp.float32)
    ).astype(jnp.bfloat16)
    stacked = jnp.concatenate([both[:, j * wide:(j + 1) * wide] for j in range(NB)], axis=0)
    packed = f32_dot(unpack, stacked, ((0,), (0,))).astype(jnp.bfloat16)
    ret_send[...] = packed.reshape(experts, HOP, wide)

    def give_back(k, _):
        dst = far(experts - k)
        pltpu.make_async_remote_copy(
            src_ref=ret_send.at[dst],
            dst_ref=ret_recv.at[chip],
            send_sem=ret_ssem,
            recv_sem=ret_rsem,
            device_id={"expert": 2 * dst + core},
        ).start()
        return 0

    lax.fori_loop(1, experts, give_back, 0)
    ret_recv[chip] = ret_send[chip]

    gate_copy.wait()
    total = gate_out[0:1, :cap] + gate_in[0:1, :cap]
    gate_ref[0] = jnp.where(core == 0, total[:, :half], total[:, half:])
    fwd_x.wait_send()
    fwd_g.wait_send()

    every = pl.ds(0, experts - 1)
    pltpu.make_async_copy(ret_recv.at[every], ret_recv.at[every], ret_rsem).wait()
    folded = f32_dot(pick, ret_recv[...].reshape(tall, wide), ((0,), (0,))).astype(jnp.bfloat16)
    for j in range(NB):
        in_grad_ref[:, j * wide:(j + 1) * wide] = folded[j * tok:(j + 1) * tok]
    for copy in keep:
        copy.wait()
    for a in range(2):
        pltpu.make_async_copy(send.at[a, every], send.at[a, every], send_sem.at[a]).wait()
    pltpu.make_async_copy(ret_send.at[every], ret_send.at[every], ret_ssem).wait()


def grads_kernel(
    rows_ref, pg_ref, hidden_ref, scaled_ref, in_grad_in, gate_in,
    up_ref, down_ref, in_grad_ref, gate_ref,
):
    @pl.when(pl.program_id(0) == 0)
    def _():
        in_grad_ref[...] = in_grad_in[...]
        gate_ref[...] = gate_in[...]

    up_ref[0] = f32_dot(rows_ref[...], pg_ref[...], ((0,), (0,))).astype(jnp.bfloat16)
    down_ref[0] = f32_dot(hidden_ref[...], scaled_ref[...], ((0,), (0,))).astype(jnp.bfloat16)


def on_device_pairs(tokens_in, out_grad, chosen, counts, gates, w_up, w_down):
    tok, width = tokens_in.shape
    experts, cap = chosen.shape[1:]
    ff = w_up.shape[2]
    rows = 2 * experts
    wide = width // NB
    bf16, f32 = jnp.bfloat16, jnp.float32
    vmem = pl.BlockSpec(memory_space=pltpu.VMEM)
    hbm = pl.BlockSpec(memory_space=pltpu.HBM)
    dma = pltpu.SemaphoreType.DMA
    in_grad, gate_grad, x_rows, scaled, hidden, pre_grad = pl.pallas_call(
        expert_kernel,
        out_shape=(
            jax.ShapeDtypeStruct((tok, width), bf16),
            jax.ShapeDtypeStruct((1, 1, cap // 2), f32),
            jax.ShapeDtypeStruct((2 * rows, width), bf16),
            jax.ShapeDtypeStruct((2 * rows, width), bf16),
            jax.ShapeDtypeStruct((2 * rows, ff), bf16),
            jax.ShapeDtypeStruct((2 * rows, ff), bf16),
        ),
        in_specs=[hbm] * 7,
        out_specs=(vmem,) * 2 + (hbm,) * 4,
        scratch_shapes=[
            pltpu.VMEM((2 * rows, width), bf16),
            pltpu.VMEM((2 * rows, width), bf16),
            pltpu.VMEM((2 * rows, ff), bf16),
            pltpu.VMEM((2 * rows, ff), bf16),
            pltpu.VMEM((tok, width), bf16),
            pltpu.VMEM((tok, width), bf16),
            pltpu.VMEM(chosen.shape, jnp.int32),
            pltpu.VMEM(counts.shape, jnp.int32),
            pltpu.VMEM(gates.shape, bf16),
            pltpu.VMEM((width, ff), bf16),
            pltpu.VMEM((ff, width), bf16),
            pltpu.VMEM((2, experts, HOP, wide), bf16),
            pltpu.VMEM((2, 2, experts, HOP, wide), bf16),
            pltpu.VMEM((2 * rows, width), bf16),
            pltpu.VMEM((2 * rows, ff), f32),
            pltpu.VMEM((2 * rows, width), f32),
            pltpu.VMEM((rows, width), bf16),
            pltpu.VMEM((rows, width), bf16),
            pltpu.VMEM((8, 128), f32),
            pltpu.VMEM((8, 128), f32),
            pltpu.VMEM((experts, HOP, wide), bf16),
            pltpu.VMEM((experts, HOP, wide), bf16),
            dma((5,)),
            dma((4,)),
            dma((2,)),
            dma((2,)),
            dma((2,)),
            dma((2,)),
            dma((2,)),
            dma,
            dma,
            dma((2,)),
            dma((2,)),
        ],
        compiler_params=pltpu.CompilerParams(
            collective_id=0, has_side_effects=True, vmem_limit_bytes=62 << 20
        ),
        cost_estimate=pl.CostEstimate(
            flops=6 * 2 * rows * width * ff,
            bytes_accessed=4 * width * ff,
            transcendentals=2 * rows * ff,
        ),
    )(tokens_in, out_grad, chosen, counts, gates, w_up, w_down)

    steps = 4
    grad_up, grad_down, in_grad, gate_grad = pl.pallas_call(
        grads_kernel,
        grid=(steps,),
        out_shape=(
            jax.ShapeDtypeStruct((1, width, ff), bf16),
            jax.ShapeDtypeStruct((1, ff, width), bf16),
            jax.ShapeDtypeStruct((tok, width), bf16),
            jax.ShapeDtypeStruct((1, 1, cap // 2), f32),
        ),
        in_specs=[
            pl.BlockSpec((2 * rows, width // steps), lambda i: (0, i)),
            pl.BlockSpec((2 * rows, ff), lambda i: (0, 0)),
            pl.BlockSpec((2 * rows, ff // steps), lambda i: (0, i)),
            pl.BlockSpec((2 * rows, width), lambda i: (0, 0)),
            pl.BlockSpec((tok, width), lambda i: (0, 0)),
            pl.BlockSpec((1, 1, cap // 2), lambda i: (0, 0, 0)),
        ],
        out_specs=(
            pl.BlockSpec((1, width // steps, ff), lambda i: (0, i, 0)),
            pl.BlockSpec((1, ff // steps, width), lambda i: (0, i, 0)),
            pl.BlockSpec((tok, width), lambda i: (0, 0)),
            pl.BlockSpec((1, 1, cap // 2), lambda i: (0, 0, 0)),
        ),
        compiler_params=pltpu.CompilerParams(vmem_limit_bytes=62 << 20),
        cost_estimate=pl.CostEstimate(
            flops=8 * rows * width * ff,
            bytes_accessed=4 * width * ff,
            transcendentals=0,
        ),
    )(x_rows, pre_grad, hidden, scaled, in_grad, gate_grad)
    return in_grad, grad_up, grad_down, gate_grad


def on_device(mesh, *args):
    tok, width = args[0].shape
    experts, cap = args[2].shape[1:]
    two = lambda v: v & (v - 1) == 0
    fits = (
        mesh.shape["dp"] == 1
        and mesh.shape["expert"] == 2 * experts
        and cap == 4 * experts
        and cap <= 128
        and tok % 16 == 0
        and width % 2048 == 0
        and args[5].shape[2] % 2048 == 0
        and two(tok)
        and two(experts)
    )
    return (on_device_pairs if fits else on_device_any)(*args)


def solution(mesh):
    placed = (
        P(("dp", "expert"), None),
        P(("dp", "expert"), None),
        P("dp", None, None),
        P("dp", None),
        P("dp", None, None),
        P("expert", None, "dp"),
        P("expert", "dp", None),
    )
    return jax.shard_map(
        functools.partial(on_device, mesh),
        mesh=mesh,
        in_specs=placed,
        out_specs=(
            P(("dp", "expert"), None),
            P("expert", None, "dp"),
            P("expert", "dp", None),
            P("dp", "expert", None),
        ),
        check_vma=False,
    )
```

```python
import functools
import jax
import jax.numpy as jnp
from jax import lax
from jax.experimental import pallas as pl
from jax.experimental.pallas import tpu as pltpu
from jax.sharding import PartitionSpec as P

root_two_over_pi = 0.7978845608028654
cubic_coef = 0.044715


def partner(x, axis, apart):
    return lax.ppermute(x, axis, [(i, i ^ 1 << apart) for i in range(lax.axis_size(axis))])


def gelu_pair(pre_act):
    inner_arg = root_two_over_pi * (pre_act + cubic_coef * pre_act * pre_act * pre_act)
    tangent = jnp.tanh(inner_arg)
    act_value = 0.5 * pre_act * (1.0 + tangent)
    act_slope = 0.5 * (1.0 + tangent) + 0.5 * pre_act * (
        1.0 - tangent * tangent
    ) * root_two_over_pi * (1.0 + 3.0 * cubic_coef * pre_act * pre_act)
    return (act_value, act_slope)


def on_device_any(tokens_in, out_grad, chosen, counts, gates, w_up, w_down):
    tok_local = tokens_in.shape[0]
    width = tokens_in.shape[1]
    owners = lax.axis_size("expert")
    groups = lax.axis_size("dp")
    capacity = chosen.shape[2]
    half_cap = capacity // 2
    num_experts = chosen.shape[1]
    device = lax.axis_index("expert")
    expert = device // 2
    parity = device % 2
    highest = lax.Precision.HIGHEST
    my_lists = chosen[0]
    slot_ids = jnp.arange(capacity, dtype=jnp.int32)
    is_valid = slot_ids[None, :] < counts[0][:, None]
    owner_of = my_lists // tok_local
    local_of = my_lists % tok_local
    mine = jnp.logical_and(owner_of == device, is_valid)
    local_ids = jnp.arange(tok_local, dtype=jnp.int32)
    hits = jnp.logical_and(mine[:, :, None], local_of[:, :, None] == local_ids[None, None, :])
    picked = jnp.sum(hits.astype(jnp.float32).reshape(num_experts, 2, half_cap, tok_local), axis=2)
    picked_low = picked.astype(jnp.bfloat16)
    list_row = lax.dynamic_index_in_dim(my_lists, expert, 0, keepdims=False)
    count_here = lax.dynamic_index_in_dim(counts[0], expert, 0, keepdims=False)
    valid_here = slot_ids < count_here
    gate_here = jnp.where(
        valid_here,
        lax.dynamic_index_in_dim(gates[0], expert, 0, keepdims=False),
        jnp.zeros((), jnp.bfloat16),
    )
    owner_ids = jnp.arange(owners, dtype=jnp.int32)
    slot_map = jnp.logical_and(
        (list_row // tok_local)[:, None] == owner_ids[None, :], valid_here[:, None]
    )
    slot_map = slot_map.astype(jnp.float32).reshape(2, half_cap, owners)
    map_low = slot_map.astype(jnp.bfloat16)
    gate_rows = gate_here.reshape(2, half_cap)
    send_x = jnp.einsum(
        "erl,ld->red", picked_low, tokens_in, preferred_element_type=jnp.float32
    ).astype(jnp.bfloat16)
    send_g = jnp.einsum(
        "erl,ld->red", picked_low, out_grad, preferred_element_type=jnp.float32
    ).astype(jnp.bfloat16)
    send_x = jnp.repeat(send_x, 2, axis=1)
    send_g = jnp.repeat(send_g, 2, axis=1)
    recv_x, recv_g = (
        lax.all_to_all(send_x, "expert", split_axis=1, concat_axis=1, tiled=True),
        lax.all_to_all(send_g, "expert", split_axis=1, concat_axis=1, tiled=True),
    )
    rows_x = jnp.einsum("rij,rjd->rid", map_low, recv_x, preferred_element_type=jnp.float32).astype(
        jnp.bfloat16
    )
    rows_g = jnp.einsum("rij,rjd->rid", map_low, recv_g, preferred_element_type=jnp.float32).astype(
        jnp.bfloat16
    )
    all_x, all_g, all_gate = (
        lax.all_gather(rows_x, "dp", axis=1, tiled=True),
        lax.all_gather(rows_g, "dp", axis=1, tiled=True),
        lax.all_gather(gate_rows, "dp", axis=1, tiled=True),
    )
    flat_x = all_x.reshape(-1, width)
    flat_g = all_g.reshape(-1, width)
    flat_gate = all_gate.reshape(-1).astype(jnp.float32)
    up_part = w_up[0]
    down_part = w_down[0]
    pre_act = jnp.dot(flat_x, up_part, preferred_element_type=jnp.float32)
    act_value, act_slope = gelu_pair(pre_act)
    hidden = act_value.astype(jnp.bfloat16)
    back_grad = lax.dot_general(
        flat_g, down_part, (((1,), (1,)), ((), ())), preferred_element_type=jnp.float32
    )
    gate_terms = jnp.sum(hidden.astype(jnp.float32) * back_grad, axis=1)
    scaled = (flat_gate[:, None] * flat_g.astype(jnp.float32)).astype(jnp.bfloat16)
    pre_grad = (flat_gate[:, None] * back_grad * act_slope).astype(jnp.bfloat16)
    grad_down = lax.dot_general(
        hidden, scaled, (((0,), (0,)), ((), ())), preferred_element_type=jnp.float32
    )
    grad_up = lax.dot_general(
        flat_x, pre_grad, (((0,), (0,)), ((), ())), preferred_element_type=jnp.float32
    )
    dx_terms = lax.dot_general(
        pre_grad, up_part, (((1,), (1,)), ((), ())), preferred_element_type=jnp.float32
    )
    hidden_sum, gate_sums = (
        lax.psum_scatter(
            dx_terms.reshape(2, groups * half_cap, width).astype(jnp.bfloat16),
            "dp",
            scatter_dimension=1,
            tiled=True,
        ).astype(jnp.float32),
        lax.psum_scatter(
            gate_terms.reshape(2, groups * half_cap).astype(jnp.bfloat16),
            "dp",
            scatter_dimension=1,
            tiled=True,
        ).astype(jnp.float32),
    )
    spread = jnp.einsum("rij,rid->rjd", slot_map, hidden_sum, precision=highest)
    returned = lax.all_to_all(
        spread.astype(jnp.bfloat16), "expert", split_axis=1, concat_axis=1, tiled=True
    ).astype(spread.dtype)
    take_back = jnp.repeat(picked, 2, axis=0)
    in_grad = jnp.einsum("krl,rkd->ld", take_back, returned, precision=highest)
    partner_gate = partner(gate_sums, "expert", 0)
    gate_total = gate_sums + partner_gate
    gate_out = lax.dynamic_index_in_dim(gate_total, parity, 0, keepdims=False).reshape(
        1, 1, half_cap
    )
    return (
        in_grad.astype(jnp.bfloat16),
        grad_up.astype(jnp.bfloat16)[None],
        grad_down.astype(jnp.bfloat16)[None],
        gate_out,
    )


NB = 8
HOP = 2 * NB


def is_one(cond):
    return jnp.where(cond, 1.0, 0.0)


def iota(shape, dim):
    return lax.broadcasted_iota(jnp.int32, shape, dim)


def f32_dot(a, b, dims=((1,), (0,))):
    return lax.dot_general(a, b, (dims, ((), ())), preferred_element_type=jnp.float32)


def expert_kernel(
    x_hbm, g_hbm, chosen_hbm, counts_hbm, gates_hbm, up_hbm, down_hbm,
    in_grad_ref, gate_ref, rows_hbm, scaled_hbm, hidden_hbm, pg_hbm,
    rows_ref, scaled_ref, hidden_ref, pg_ref, x_ref, g_ref, chosen_ref, counts_ref, gates_ref, up_v, down_v, send, recv, grows, slope, dx_acc, dx_out, dx_in, gate_out, gate_in,
    ret_send, ret_recv,
    in_sem, out_sem, w_sem, send_sem, recv_sem, fwd_send, fwd_recv, ret_ssem, ret_rsem, pair_send, pair_recv,
):
    tok, width = x_ref.shape
    experts, cap = chosen_ref.shape[1:]
    ff = up_v.shape[1]
    half = cap // 2
    wide = width // NB
    rows = 2 * experts
    log_tok = tok.bit_length() - 1
    me = lax.axis_index("expert")
    chip = me // 2
    core = me % 2
    mate = me + 1 - 2 * core

    small = [
        pltpu.make_async_copy(src, dst, in_sem.at[i])
        for i, (src, dst) in enumerate(
            (
                (chosen_hbm, chosen_ref),
                (counts_hbm, counts_ref),
                (x_hbm, x_ref),
                (g_hbm, g_ref),
                (gates_hbm, gates_ref),
            )
        )
    ]
    for copy in small:
        copy.start()
    up_copy = pltpu.make_async_copy(up_hbm.at[0], up_v, w_sem.at[0])
    down_copy = pltpu.make_async_copy(down_hbm.at[0], down_v, w_sem.at[1])
    up_copy.start()
    down_copy.start()

    def far(k):
        return lax.rem(chip + k, experts)

    barrier = pltpu.get_barrier_semaphore()
    pl.semaphore_signal(barrier, inc=1, device_id={"expert": mate})

    def greet(k, _):
        pl.semaphore_signal(barrier, inc=1, device_id={"expert": 2 * far(k) + core})
        return 0

    lax.fori_loop(1, experts, greet, 0)

    small[0].wait()
    small[1].wait()

    chosen = chosen_ref[0]
    slot = iota((experts, cap), 1)
    counts = counts_ref[...].astype(jnp.float32)
    diag = iota((experts, experts), 0) == iota((experts, experts), 1)
    count_col = jnp.sum(jnp.where(diag, counts, 0.0), axis=1, keepdims=True)
    local = chosen - me * tok
    mine = (local >= 0) & (local < tok) & (slot.astype(jnp.float32) < count_col)
    local_one = local.astype(jnp.float32) + 1.0
    lanes = NB * tok
    named = jnp.concatenate(
        [
            jnp.broadcast_to(
                jnp.sum(
                    jnp.where(mine & ((slot >= half) == bool(r)), local_one, 0.0),
                    axis=1, keepdims=True,
                ),
                (experts, lanes),
            )
            for r in range(2)
        ],
        axis=0,
    ).astype(jnp.bfloat16)
    tall = experts * HOP
    ti, tc = iota((tall, rows), 0), iota((tall, rows), 1)
    want = (ti & (HOP - 1)) // NB * experts + ti // HOP
    spread = is_one(want == tc).astype(jnp.bfloat16)
    full = f32_dot(spread, named)
    qi, ql = iota((tall, lanes), 0), iota((tall, lanes), 1)
    pick = is_one(
        (full == ((ql & (tok - 1)) + 1).astype(jnp.float32))
        & ((qi & (NB - 1)) == (ql >> log_tok))
    ).astype(jnp.bfloat16)

    small[2].wait()
    pl.semaphore_wait(barrier, experts)

    for a, ref in enumerate((x_ref, g_ref)):
        if a == 1:
            small[3].wait()
        stacked = jnp.concatenate(
            [ref[:, j * wide:(j + 1) * wide] for j in range(NB)], axis=0
        )
        packed = f32_dot(pick, stacked).astype(jnp.bfloat16)
        send[a] = packed.reshape(experts, HOP, wide)

        def push(k, _, a=a):
            dst = far(experts - k)
            pltpu.make_async_remote_copy(
                src_ref=send.at[a, dst],
                dst_ref=recv.at[a, core, chip],
                send_sem=send_sem.at[a],
                recv_sem=recv_sem.at[a],
                device_id={"expert": 2 * dst + core},
            ).start()
            return 0

        lax.fori_loop(1, experts, push, 0)
        recv[a, core, chip] = send[a, chip]

    pi, pc = iota((tall, tall), 0), iota((tall, tall), 1)
    unpack = is_one(
        pc == ((pi & (rows - 1)) >> 1) * HOP + (pi & 1) * NB + pi // rows
    ).astype(jnp.bfloat16)

    def arrive(a):
        every = pl.ds(0, experts - 1)
        pltpu.make_async_copy(
            recv.at[a, core, every], recv.at[a, core, every], recv_sem.at[a]
        ).wait()
        copy = pltpu.make_async_remote_copy(
            src_ref=recv.at[a, core],
            dst_ref=recv.at[a, core],
            send_sem=fwd_send.at[a],
            recv_sem=fwd_recv.at[a],
            device_id={"expert": mate},
        )
        copy.start()
        return copy

    def unfold(a, parity, out):
        flat = f32_dot(unpack, recv[a, parity].reshape(tall, wide)).astype(jnp.bfloat16)
        at = pl.ds(pl.multiple_of(parity * rows, rows), rows)
        for j in range(NB):
            out[at, j * wide:(j + 1) * wide] = flat[j * rows:(j + 1) * rows]

    def other_half(a):
        return pltpu.make_async_remote_copy(
            src_ref=recv.at[a, 1 - core],
            dst_ref=recv.at[a, 1 - core],
            send_sem=fwd_send.at[a],
            recv_sem=fwd_recv.at[a],
            device_id={"expert": mate},
        )

    small[4].wait()

    my_list = chosen_ref[0, pl.ds(chip, 1), :]
    my_gate = gates_ref[0].astype(jnp.float32)
    my_gate = jnp.sum(
        jnp.where(iota((experts, cap), 0) == chip, my_gate, 0.0), axis=0, keepdims=True
    )
    my_count = jnp.sum(
        jnp.where(iota((1, experts), 1) == chip, counts, 0.0), axis=1, keepdims=True
    )
    owner = my_list >> log_tok
    late = jnp.where(iota((1, cap), 1) >= half, 1, 0)
    place = (owner & 1) * rows + (owner >> 1) * 2 + late
    live = iota((1, cap), 1).astype(jnp.float32) < my_count
    seat = is_one((iota((2 * rows, cap), 0) == place) & live)
    weight = jnp.sum(seat * my_gate, axis=1, keepdims=True)

    fwd_x = arrive(0)
    unfold(0, core, rows_ref)
    up_copy.wait()
    other_half(0).wait_recv()
    unfold(0, 1 - core, rows_ref)

    step = 1024
    x_rows = rows_ref[...]

    def forward(c, _):
        cols = pl.ds(pl.multiple_of(c * step, step), step)
        value, tilt = gelu_pair(f32_dot(x_rows, up_v[:, cols]))
        hidden_ref[:, cols] = value.astype(jnp.bfloat16)
        slope[:, cols] = tilt
        return 0

    lax.fori_loop(0, ff // step, forward, 0)

    fwd_g = arrive(1)
    unfold(1, core, grows)
    down_copy.wait()
    other_half(1).wait_recv()
    unfold(1, 1 - core, grows)
    g_rows = grows[...]
    scaled_ref[...] = (weight * g_rows.astype(jnp.float32)).astype(jnp.bfloat16)

    def backward(c, total):
        cols = pl.ds(pl.multiple_of(c * step, step), step)
        back = f32_dot(g_rows, down_v[cols, :], ((1,), (1,)))
        pre_grad = (weight * back * slope[:, cols]).astype(jnp.bfloat16)
        pg_ref[:, cols] = pre_grad
        return total + jnp.sum(
            hidden_ref[:, cols].astype(jnp.float32) * back, axis=1, keepdims=True
        )

    gate_terms = lax.fori_loop(
        0, ff // step, backward, jnp.zeros((2 * rows, 1), jnp.float32)
    )

    theirs = pl.ds(pl.multiple_of((1 - core) * rows, rows), rows)
    ours = pl.ds(pl.multiple_of(core * rows, rows), rows)
    low = gate_terms.astype(jnp.bfloat16).astype(jnp.float32)
    by_slot = jnp.sum(seat * low, axis=0, keepdims=True)
    gate_out[...] = jnp.broadcast_to(
        jnp.concatenate([by_slot, jnp.zeros((1, 128 - cap), jnp.float32)], axis=1), (8, 128)
    )
    gate_copy = pltpu.make_async_remote_copy(
        src_ref=gate_out, dst_ref=gate_in,
        send_sem=pair_send.at[2], recv_sem=pair_recv.at[2], device_id={"expert": mate},
    )
    gate_copy.start()
    keep = [
        pltpu.make_async_copy(src, dst, out_sem.at[i])
        for i, (src, dst) in enumerate(
            (
                (rows_ref, rows_hbm),
                (scaled_ref, scaled_hbm),
                (hidden_ref, hidden_hbm),
                (pg_ref, pg_hbm),
            )
        )
    ]
    for copy in keep:
        copy.start()
    part = width // 2
    thin = part // NB
    dx_copies = []
    for h in range(2):
        cols = slice(h * part, (h + 1) * part)
        dx_acc[:, cols] = f32_dot(pg_ref[...], up_v[cols, :], ((1,), (1,)))
        dx_out[h] = dx_acc[theirs, cols].astype(jnp.bfloat16)
        copy = pltpu.make_async_remote_copy(
            src_ref=dx_out.at[h], dst_ref=dx_in.at[h],
            send_sem=pair_send.at[h], recv_sem=pair_recv.at[h], device_id={"expert": mate},
        )
        copy.start()
        dx_copies.append(copy)
    for h in range(2):
        cols = slice(h * part, (h + 1) * part)
        dx_copies[h].wait()
        both = (
            dx_acc[ours, cols].astype(jnp.bfloat16).astype(jnp.float32)
            + dx_in[h].astype(jnp.float32)
        ).astype(jnp.bfloat16)
        stacked = jnp.concatenate(
            [both[:, j * thin:(j + 1) * thin] for j in range(NB)], axis=0
        )
        packed = f32_dot(unpack, stacked, ((0,), (0,))).astype(jnp.bfloat16)
        ret_send[h] = packed.reshape(experts, HOP, thin)

        def give_back(k, _, h=h):
            dst = far(experts - k)
            pltpu.make_async_remote_copy(
                src_ref=ret_send.at[h, dst],
                dst_ref=ret_recv.at[h, chip],
                send_sem=ret_ssem.at[h],
                recv_sem=ret_rsem.at[h],
                device_id={"expert": 2 * dst + core},
            ).start()
            return 0

        lax.fori_loop(1, experts, give_back, 0)
        ret_recv[h, chip] = ret_send[h, chip]

    gate_copy.wait()
    total = gate_out[0:1, :cap] + gate_in[0:1, :cap]
    gate_ref[0] = jnp.where(core == 0, total[:, :half], total[:, half:])
    fwd_x.wait_send()
    fwd_g.wait_send()

    every = pl.ds(0, experts - 1)
    for h in range(2):
        pltpu.make_async_copy(
            ret_recv.at[h, every], ret_recv.at[h, every], ret_rsem.at[h]
        ).wait()
        folded = f32_dot(
            pick, ret_recv[h].reshape(tall, thin), ((0,), (0,))
        ).astype(jnp.bfloat16)
        for j in range(NB):
            at = h * part + j * thin
            in_grad_ref[:, at:at + thin] = folded[j * tok:(j + 1) * tok]
    for copy in keep:
        copy.wait()
    for a in range(2):
        pltpu.make_async_copy(send.at[a, every], send.at[a, every], send_sem.at[a]).wait()
        pltpu.make_async_copy(
            ret_send.at[a, every], ret_send.at[a, every], ret_ssem.at[a]
        ).wait()


def grads_kernel(
    rows_ref, pg_ref, hidden_ref, scaled_ref, in_grad_in, gate_in,
    up_ref, down_ref, in_grad_ref, gate_ref,
):
    @pl.when(pl.program_id(0) == 0)
    def _():
        in_grad_ref[...] = in_grad_in[...]
        gate_ref[...] = gate_in[...]

    up_ref[0] = f32_dot(rows_ref[...], pg_ref[...], ((0,), (0,))).astype(jnp.bfloat16)
    down_ref[0] = f32_dot(hidden_ref[...], scaled_ref[...], ((0,), (0,))).astype(jnp.bfloat16)


def on_device_pairs(tokens_in, out_grad, chosen, counts, gates, w_up, w_down):
    tok, width = tokens_in.shape
    experts, cap = chosen.shape[1:]
    ff = w_up.shape[2]
    rows = 2 * experts
    wide = width // NB
    bf16, f32 = jnp.bfloat16, jnp.float32
    vmem = pl.BlockSpec(memory_space=pltpu.VMEM)
    hbm = pl.BlockSpec(memory_space=pltpu.HBM)
    dma = pltpu.SemaphoreType.DMA
    in_grad, gate_grad, x_rows, scaled, hidden, pre_grad = pl.pallas_call(
        expert_kernel,
        out_shape=(
            jax.ShapeDtypeStruct((tok, width), bf16),
            jax.ShapeDtypeStruct((1, 1, cap // 2), f32),
            jax.ShapeDtypeStruct((2 * rows, width), bf16),
            jax.ShapeDtypeStruct((2 * rows, width), bf16),
            jax.ShapeDtypeStruct((2 * rows, ff), bf16),
            jax.ShapeDtypeStruct((2 * rows, ff), bf16),
        ),
        in_specs=[hbm] * 7,
        out_specs=(vmem,) * 2 + (hbm,) * 4,
        scratch_shapes=[
            pltpu.VMEM((2 * rows, width), bf16),
            pltpu.VMEM((2 * rows, width), bf16),
            pltpu.VMEM((2 * rows, ff), bf16),
            pltpu.VMEM((2 * rows, ff), bf16),
            pltpu.VMEM((tok, width), bf16),
            pltpu.VMEM((tok, width), bf16),
            pltpu.VMEM(chosen.shape, jnp.int32),
            pltpu.VMEM(counts.shape, jnp.int32),
            pltpu.VMEM(gates.shape, bf16),
            pltpu.VMEM((width, ff), bf16),
            pltpu.VMEM((ff, width), bf16),
            pltpu.VMEM((2, experts, HOP, wide), bf16),
            pltpu.VMEM((2, 2, experts, HOP, wide), bf16),
            pltpu.VMEM((2 * rows, width), bf16),
            pltpu.VMEM((2 * rows, ff), f32),
            pltpu.VMEM((2 * rows, width), f32),
            pltpu.VMEM((2, rows, width // 2), bf16),
            pltpu.VMEM((2, rows, width // 2), bf16),
            pltpu.VMEM((8, 128), f32),
            pltpu.VMEM((8, 128), f32),
            pltpu.VMEM((2, experts, HOP, wide // 2), bf16),
            pltpu.VMEM((2, experts, HOP, wide // 2), bf16),
            dma((5,)),
            dma((4,)),
            dma((2,)),
            dma((2,)),
            dma((2,)),
            dma((2,)),
            dma((2,)),
            dma((2,)),
            dma((2,)),
            dma((3,)),
            dma((3,)),
        ],
        compiler_params=pltpu.CompilerParams(
            collective_id=0, has_side_effects=True, vmem_limit_bytes=62 << 20
        ),
        cost_estimate=pl.CostEstimate(
            flops=6 * 2 * rows * width * ff,
            bytes_accessed=4 * width * ff,
            transcendentals=2 * rows * ff,
        ),
    )(tokens_in, out_grad, chosen, counts, gates, w_up, w_down)

    steps = 4
    grad_up, grad_down, in_grad, gate_grad = pl.pallas_call(
        grads_kernel,
        grid=(steps,),
        out_shape=(
            jax.ShapeDtypeStruct((1, width, ff), bf16),
            jax.ShapeDtypeStruct((1, ff, width), bf16),
            jax.ShapeDtypeStruct((tok, width), bf16),
            jax.ShapeDtypeStruct((1, 1, cap // 2), f32),
        ),
        in_specs=[
            pl.BlockSpec((2 * rows, width // steps), lambda i: (0, i)),
            pl.BlockSpec((2 * rows, ff), lambda i: (0, 0)),
            pl.BlockSpec((2 * rows, ff // steps), lambda i: (0, i)),
            pl.BlockSpec((2 * rows, width), lambda i: (0, 0)),
            pl.BlockSpec((tok, width), lambda i: (0, 0)),
            pl.BlockSpec((1, 1, cap // 2), lambda i: (0, 0, 0)),
        ],
        out_specs=(
            pl.BlockSpec((1, width // steps, ff), lambda i: (0, i, 0)),
            pl.BlockSpec((1, ff // steps, width), lambda i: (0, i, 0)),
            pl.BlockSpec((tok, width), lambda i: (0, 0)),
            pl.BlockSpec((1, 1, cap // 2), lambda i: (0, 0, 0)),
        ),
        compiler_params=pltpu.CompilerParams(vmem_limit_bytes=62 << 20),
        cost_estimate=pl.CostEstimate(
            flops=8 * rows * width * ff,
            bytes_accessed=4 * width * ff,
            transcendentals=0,
        ),
    )(x_rows, pre_grad, hidden, scaled, in_grad, gate_grad)
    return in_grad, grad_up, grad_down, gate_grad


def on_device(mesh, *args):
    tok, width = args[0].shape
    experts, cap = args[2].shape[1:]
    two = lambda v: v & (v - 1) == 0
    fits = (
        mesh.shape["dp"] == 1
        and mesh.shape["expert"] == 2 * experts
        and cap == 4 * experts
        and cap <= 128
        and tok % 16 == 0
        and width % 2048 == 0
        and args[5].shape[2] % 2048 == 0
        and two(tok)
        and two(experts)
    )
    return (on_device_pairs if fits else on_device_any)(*args)


def solution(mesh):
    placed = (
        P(("dp", "expert"), None),
        P(("dp", "expert"), None),
        P("dp", None, None),
        P("dp", None),
        P("dp", None, None),
        P("expert", None, "dp"),
        P("expert", "dp", None),
    )
    return jax.shard_map(
        functools.partial(on_device, mesh),
        mesh=mesh,
        in_specs=placed,
        out_specs=(
            P(("dp", "expert"), None),
            P("expert", None, "dp"),
            P("expert", "dp", None),
            P("dp", "expert", None),
        ),
        check_vma=False,
    )
```
